32 devices in a mesh: parts: 1, loop: 32 (over z, y, x, core).
Axes of the slice: x: 2, y: 2, z: 4, core: 2. Of those that a mesh axis runs over, the one named last changes fastest.
Arguments:
- slots: bfloat16 [2048, 4096], P(('parts', 'loop')), may hold values from -6 to 6
- tile_expert: int32 [16, 1], P('parts'), may hold values from 0 to 1
- slot_weight: float32 [2048], P(('parts', 'loop')), may hold values from 0.2 to 1
- gate_weight: bfloat16 [2, 4096, 12288], P(None, None, 'loop'), may hold values from -0.09375 to 0.09375
- up_weight: bfloat16 [2, 4096, 12288], P(None, None, 'loop'), may hold values from -0.09375 to 0.09375
- down_weight: bfloat16 [2, 12288, 4096], P(None, 'loop'), may hold values from -0.0546875 to 0.0546875
Outputs:
- expert_out: bfloat16 [2048, 4096], P(('parts', 'loop'))
The draws below stay inside these ranges and needn't reach their ends.
Inputs may be any that keep to these rules, and one draw needn't show every extreme that they name: `tile_expert`: each block names one expert; every expert is named by some block.
All inputs are finite; a program needn't handle non-finite values.
Results may differ from the reference program's by a relative error of at most 0.0049.
Values may be sent and summed in bfloat16 or wider, within the bound.
A program may use at most 256 MiB of HBM per device.

```python
import math
import jax
import jax.numpy as jnp
from jax import lax

D = 4096
FFW = 12288
EXPW = 2
TILE = 128
SLOTS = 2048
TILES = 16


def shard_levels(stream_key, dims, pieces, low, top_value):
    loudness, own = 1.0, jax.random.fold_in(stream_key, 6)
    for position, parts in pieces:
        steps = jnp.exp(jax.random.uniform(jax.random.fold_in(own, position), (parts,), jnp.float32, low / len(pieces), top_value / len(pieces)))
        loudness = loudness * jnp.repeat(steps, dims[position] // parts).reshape([-1 if axis == position else 1 for axis in range(len(dims))])
    return loudness


def distinct(rng, rows, count, top, lift):
    ranking = jax.random.permutation(jax.random.fold_in(rng, 1), count)
    pull = ranking
    for power in range(3):
        pull = pull * pull // count
    pull = pull * lift // count
    chance = jax.random.randint(jax.random.fold_in(rng, 2), (rows, count), 0, 4096) + pull
    sure = jax.random.permutation(jax.random.fold_in(rng, 3), rows)[jnp.arange(count) % rows]
    chance = jnp.where(jnp.arange(rows)[:, None] == sure[None, :], 1 << 14, chance)
    merit = chance * count + jnp.arange(count)
    return lax.top_k(merit.astype(jnp.int32), top)[1].astype(jnp.int32)


def normal_values(own_key, shape, deviation, reach, shards=(), dtype=jnp.bfloat16):
    loudness = shard_levels(own_key, shape, shards, -0.22, 0.18) if shards else 1.0
    drawn = jax.random.normal(own_key, shape, jnp.float32) * deviation * loudness
    return jnp.minimum(jnp.maximum(drawn, -reach), reach).astype(dtype)


def setup_inputs(seed: int = 0, part: int = 0) -> dict:
    arg_keys = jax.random.split(jax.random.key(seed), 7)
    part_keys = jax.random.split(jax.random.fold_in(arg_keys[6], part), 7)
    return {
        "slots": normal_values(part_keys[0], (SLOTS, D), 1.0, 6.0, ((0, 32),)),
        "tile_expert": distinct(part_keys[1], TILES, EXPW, 1, 0),
        "slot_weight": jnp.clip(jnp.exp(math.log(1.0) - 1.609438 * jax.random.uniform(part_keys[2], (SLOTS,), jnp.float32) ** shard_levels(part_keys[2], (SLOTS,), ((0, 32),), -0.2, 0.2)), 0.2, 1.0),
        "gate_weight": normal_values(arg_keys[3], (EXPW, D, FFW), D ** -0.5, 0.09375, ((2, 32),)),
        "up_weight": normal_values(arg_keys[4], (EXPW, D, FFW), D ** -0.5, 0.09375, ((2, 32),)),
        "down_weight": normal_values(arg_keys[5], (EXPW, FFW, D), FFW ** -0.5, 0.0546875, ((1, 32),)),
    }


def reference(slots, tile_expert, slot_weight, gate_weight, up_weight, down_weight):
    chosen_ids = tile_expert[:, 0].astype(jnp.int32)
    tile_rows = slots.reshape(-1, TILE, D)

    def expert_tile(operands):
        row_block, chosen = operands
        gate_cols = lax.dynamic_index_in_dim(gate_weight, chosen, 0, keepdims=False)
        up_cols = lax.dynamic_index_in_dim(up_weight, chosen, 0, keepdims=False)
        down_rows = lax.dynamic_index_in_dim(down_weight, chosen, 0, keepdims=False)
        gate_value = jnp.dot(row_block, gate_cols, preferred_element_type=jnp.float32)
        up_value = jnp.dot(row_block, up_cols, preferred_element_type=jnp.float32)
        hidden = (jax.nn.silu(gate_value) * up_value).astype(jnp.bfloat16)
        return jnp.dot(hidden, down_rows, preferred_element_type=jnp.float32)

    summed = lax.map(expert_tile, (tile_rows, chosen_ids)).reshape(-1, D)
    return (slot_weight[:, None] * summed).astype(jnp.bfloat16)
```

```python
import functools

import jax
import jax.numpy as jnp
from jax import lax
from jax.experimental import pallas as pl
from jax.experimental.pallas import tpu as pltpu
from jax.sharding import PartitionSpec as P

TILE = 128
MESH = pl.DeviceIdType.MESH
F32 = jnp.float32


def expert_part(row_block, chosen, gate_weight, up_weight, down_weight):
    gate_cols = lax.dynamic_index_in_dim(gate_weight, chosen, 0, keepdims=False)
    up_cols = lax.dynamic_index_in_dim(up_weight, chosen, 0, keepdims=False)
    down_rows = lax.dynamic_index_in_dim(down_weight, chosen, 0, keepdims=False)
    gate_value = jnp.dot(row_block, gate_cols, preferred_element_type=jnp.float32)
    up_value = jnp.dot(row_block, up_cols, preferred_element_type=jnp.float32)
    hidden = (jax.nn.silu(gate_value) * up_value).astype(jnp.bfloat16)
    return jnp.dot(hidden, down_rows, preferred_element_type=jnp.float32)


def collective_form(slots, tile_expert, slot_weight, gate_weight, up_weight, down_weight):
    chosen_ids = tile_expert[:, 0]
    width = slots.shape[1]
    gathered = lax.all_gather(slots, "loop", axis=0, tiled=True)
    tile_rows = gathered.reshape(-1, TILE, width)

    def expert_tile(operands):
        row_block, chosen = operands
        return expert_part(row_block, chosen, gate_weight, up_weight, down_weight)

    partial_value = lax.map(expert_tile, (tile_rows, chosen_ids)).reshape(-1, width)
    summed = lax.psum_scatter(partial_value, "loop", scatter_dimension=0, tiled=True)
    return (slot_weight[:, None] * summed).astype(jnp.bfloat16)


def kernel(nz, te, slots, gate, up, down, out, x, wgu, wd, xv, own, stage, sib, rd, rx, ry, rz,
           wsem, xsem, s_zu, s_zd, r_z, s_x, r_x, s_y, r_y, s_f, r_f, s_s, r_s,
           s_p, r_p, s_d, r_d, s_px, r_px, s_py, r_py, s_ru, s_rd, r_rz):
    rows, width = slots.shape
    half = rows // 2
    ff = gate.shape[2]
    me = lax.axis_index("loop")
    c = me % 2
    px = (me // 2) % 2
    py = (me // 4) % 2
    z = me // 8
    turn = 1 - 2 * ((2 * z) // nz)

    def chip(s, j):
        return (s * 2 + (py + j // 2) % 2) * 2 + (px + j % 2) % 2

    def device(s, j, core):
        return {"loop": chip(s, j) * 2 + core}

    xn, yn, sb = device(z, 1, c), device(z, 2, c), device(z, 0, 1 - c)

    def zdev(step):
        return {"loop": me + 8 * step}

    has_up, has_dn = z < nz - 1, z > 0

    def remote(src, dst, ssem, rsem, dev):
        return pltpu.make_async_remote_copy(src_ref=src, dst_ref=dst, send_sem=ssem, recv_sem=rsem,
                                            device_id=dev, device_id_type=MESH)

    def order(i):
        return (z + turn * i + nz) % nz

    def zu(q):
        b = x.at[chip(q, 0), c]
        return remote(b, b, s_zu.at[q], r_z.at[q], zdev(1))

    def zd(q):
        b = x.at[chip(q, 0), c]
        return remote(b, b, s_zd.at[q], r_z.at[q], zdev(-1))

    def gx(s):
        b = x.at[chip(s, 0), c]
        return remote(b, b, s_x.at[s], r_x.at[s], xn)

    def gy(s):
        b = x.at[chip(s, 0), c]
        return remote(b, b, s_y.at[s], r_y.at[s], yn)

    def fy(s):
        b = x.at[chip(s, 1), c, pl.ds(0, half)]
        return remote(b, b, s_f.at[s, 0], r_f.at[s, 0], yn)

    def fx(s):
        b = x.at[chip(s, 2), c, pl.ds(half, half)]
        return remote(b, b, s_f.at[s, 1], r_f.at[s, 1], xn)

    def gs(k):
        b = x.at[k, c]
        return remote(b, b, s_s.at[k], r_s.at[k], sb)

    def ps(k):
        return remote(stage.at[k], sib.at[k], s_p.at[k], r_p.at[k], sb)

    def dx(s):
        return remote(own.at[chip(s, 3), pl.ds(0, half)], rd.at[s, 0], s_d.at[s, 0], r_d.at[s, 0], xn)

    def dy(s):
        return remote(own.at[chip(s, 3), pl.ds(half, half)], rd.at[s, 1], s_d.at[s, 1], r_d.at[s, 1], yn)

    def sx(s):
        return remote(own.at[chip(s, 1)], rx.at[s], s_px.at[s], r_px.at[s], xn)

    def sy(s):
        return remote(own.at[chip(s, 2)], ry.at[s], s_py.at[s], r_py.at[s], yn)

    def ru(s):
        return remote(own.at[chip(s, 0)], rz.at[s], s_ru.at[s], r_rz.at[s], zdev(1))

    def rdn(s):
        slot = jnp.where(z - 1 == s, nz, s)
        return remote(own.at[chip(s, 0)], rz.at[slot], s_rd.at[s], r_rz.at[slot], zdev(-1))

    def rz_wait(slot):
        remote(rz.at[slot], rz.at[slot], s_ru.at[0], r_rz.at[slot], zdev(0)).wait_recv()

    mine = chip(z, 0)
    first = pltpu.make_async_copy(slots, x.at[mine, c], wsem.at[0])
    first.start()
    loads = [
        pltpu.make_async_copy(gate, wgu.at[:, :, pl.ds(0, ff)], wsem.at[1]),
        pltpu.make_async_copy(up, wgu.at[:, :, pl.ds(ff, ff)], wsem.at[2]),
        pltpu.make_async_copy(down, wd, wsem.at[3]),
    ]

    barrier = pltpu.get_barrier_semaphore()
    for dev in (sb, xn, yn):
        pl.semaphore_signal(barrier, inc=1, device_id=dev, device_id_type=MESH)

    @pl.when(has_up)
    def _():
        pl.semaphore_signal(barrier, inc=1, device_id=zdev(1), device_id_type=MESH)

    @pl.when(has_dn)
    def _():
        pl.semaphore_signal(barrier, inc=1, device_id=zdev(-1), device_id_type=MESH)

    pl.semaphore_wait(barrier, 3 + has_up.astype(jnp.int32) + has_dn.astype(jnp.int32))
    first.wait()

    def z_send(q, going_up):
        @pl.when(has_up if going_up else has_dn)
        def _():
            (zu if going_up else zd)(q).start()

    def stage_z(t):
        low, high = z - t, z + t

        @pl.when(low >= 0)
        def _():
            zu(low).wait_recv()
            z_send(low, True)

        @pl.when(high < nz)
        def _():
            zd(high).wait_recv()
            z_send(high, False)

    def stage_a(i):
        s = order(i)
        gx(s).start()
        gy(s).start()
        gs(chip(s, 0)).start()

    def stage_b(i):
        s = order(i)
        remote(x.at[chip(s, 1), c], x.at[chip(s, 1), c], s_x.at[s], r_x.at[s], xn).wait_recv()
        fy(s).start()
        gs(chip(s, 1)).start()
        remote(x.at[chip(s, 2), c], x.at[chip(s, 2), c], s_y.at[s], r_y.at[s], yn).wait_recv()
        fx(s).start()
        gs(chip(s, 2)).start()

    def stage_c(i):
        s = order(i)
        k = chip(s, 3)
        for h in range(2):
            b = x.at[k, c, pl.ds(h * half, half)]
            remote(b, b, s_f.at[s, h], r_f.at[s, h], xn).wait_recv()
        gs(k).start()

    def load(s, j):
        k, slot = chip(s, j), j % 2
        return [pltpu.make_async_copy(x.at[k, c], xv.at[slot, pl.ds(0, rows)], xsem.at[slot, 0]),
                pltpu.make_async_copy(x.at[k, 1 - c], xv.at[slot, pl.ds(rows, rows)], xsem.at[slot, 1])]

    def fetch(s, j):
        b = x.at[chip(s, j), 1 - c]
        remote(b, b, s_s.at[0], r_s.at[chip(s, j)], sb).wait_recv()
        for cp in load(s, j):
            cp.start()

    def stage_d(i):
        s = order(i)
        fetch(s, 0)

        def block(j, carry):
            @pl.when(j < 3)
            def _():
                fetch(s, j + 1)

            for cp in load(s, j):
                cp.wait()
            k, slot = chip(s, j), j % 2
            e = te[k, 0]
            step = min(width, 1024)
            acc = jnp.zeros((2 * rows, 2 * ff), F32)
            for k0 in range(0, width, step):
                acc += jnp.dot(xv[slot, :, k0:k0 + step], wgu[e, k0:k0 + step, :],
                               preferred_element_type=F32)
            hidden = (jax.nn.silu(acc[:, :ff]) * acc[:, ff:]).astype(jnp.bfloat16)
            for n0 in range(0, width, step):
                part = jnp.dot(hidden, wd[e, :, n0:n0 + step], preferred_element_type=F32)
                part = part.astype(jnp.bfloat16)
                own[k, :, n0:n0 + step] = part[:rows]
                stage[k, :, n0:n0 + step] = part[rows:]
            ps(k).start()
            return carry

        lax.fori_loop(0, 4, block, 0)

    def stage_r1(i):
        s = order(i)

        def add(j, carry):
            k = chip(s, 3 - j)
            ps(k).wait_recv()
            own[k] = (own[k].astype(F32) + sib[k].astype(F32)).astype(jnp.bfloat16)
            return carry

        lax.fori_loop(0, 1, add, 0)
        dx(s).start()
        dy(s).start()
        lax.fori_loop(1, 4, add, 0)

    def stage_r2(i):
        s = order(i)
        kx, ky = chip(s, 1), chip(s, 2)
        dx(s).wait_recv()
        own[ky, :half] = (own[ky, :half].astype(F32) + rd[s, 0].astype(F32)).astype(jnp.bfloat16)
        sy(s).start()
        dy(s).wait_recv()
        own[kx, half:] = (own[kx, half:].astype(F32) + rd[s, 1].astype(F32)).astype(jnp.bfloat16)
        sx(s).start()

    def stage_r3(i):
        s = order(i)
        k = chip(s, 0)
        sx(s).wait_recv()
        sy(s).wait_recv()

        @pl.when(jnp.logical_or(jnp.logical_and(s >= z, has_dn), jnp.logical_and(s < z, has_up)))
        def _():
            rz_wait(s)

        total = own[k].astype(F32) + rx[s].astype(F32) + ry[s].astype(F32) + rz[s].astype(F32)

        @pl.when(s != z)
        def _():
            own[k] = total.astype(jnp.bfloat16)

        @pl.when(s > z)
        def _():
            ru(s).start()

        @pl.when(s < z)
        def _():
            rdn(s).start()

        @pl.when(s == z)
        def _():
            @pl.when(has_up)
            def _():
                rz_wait(nz)

            out[...] = total + rz[nz].astype(F32)

    z_send(z, True)
    z_send(z, False)
    stage_a(0)
    for cp in loads:
        cp.start()

    @pl.when(jnp.logical_not(has_dn))
    def _():
        rz[pl.ds(0, nz)] = jnp.zeros((nz, rows, width), jnp.bfloat16)

    @pl.when(jnp.logical_not(has_up))
    def _():
        rz[pl.ds(0, nz - 1)] = jnp.zeros((nz - 1, rows, width), jnp.bfloat16)
        rz[nz] = jnp.zeros((rows, width), jnp.bfloat16)

    stage_z(1)
    stage_a(1)
    stage_b(0)

    def body(n, carry):
        @pl.when(n + 2 < nz)
        def _():
            stage_z(n + 2)
            stage_a(n + 2)

        @pl.when(n < nz)
        def _():
            stage_c(n)

        @pl.when(n + 1 < nz)
        def _():
            stage_b(n + 1)

        @pl.when(n == 0)
        def _():
            for cp in loads:
                cp.wait()

        @pl.when(n < nz)
        def _():
            stage_d(n)

        @pl.when(jnp.logical_and(n >= 1, n <= nz))
        def _():
            stage_r1(n % nz)

        @pl.when(jnp.logical_and(n >= 2, n <= nz + 1))
        def _():
            stage_r2((n - 1) % nz)

        @pl.when(n >= 3)
        def _():
            stage_r3((n - 2) % nz)

        return carry

    lax.fori_loop(0, nz + 3, body, 0)

    def finish(q, carry):
        for cp in (gx(q), gy(q), fx(q), fy(q), dx(q), dy(q), sx(q), sy(q)):
            cp.wait_send()

        @pl.when(jnp.logical_and(has_up, q <= z))
        def _():
            zu(q).wait_send()

        @pl.when(jnp.logical_and(has_dn, q >= z))
        def _():
            zd(q).wait_send()

        @pl.when(q > z)
        def _():
            ru(q).wait_send()

        @pl.when(q < z)
        def _():
            rdn(q).wait_send()

        return carry

    lax.fori_loop(0, nz, finish, 0)

    def finish_pair(k, carry):
        gs(k).wait_send()
        ps(k).wait_send()
        return carry

    lax.fori_loop(0, 4 * nz, finish_pair, 0)


def kernel_form(n, slots, tile_expert, slot_weight, gate_weight, up_weight, down_weight):
    nz, blocks = n // 8, n // 2
    rows, width = slots.shape
    experts, _, ff = gate_weight.shape
    bf16 = jnp.bfloat16
    dma = pltpu.SemaphoreType.DMA
    anywhere = pl.BlockSpec(memory_space=pl.ANY)
    summed, _ = pl.pallas_call(
        functools.partial(kernel, nz),
        out_shape=(jax.ShapeDtypeStruct((rows, width), F32),
                   jax.ShapeDtypeStruct((blocks, 2, rows, width), bf16)),
        in_specs=[pl.BlockSpec(memory_space=pltpu.SMEM)] + [anywhere] * 4,
        out_specs=(pl.BlockSpec(memory_space=pltpu.VMEM), anywhere),
        scratch_shapes=[
            pltpu.VMEM((experts, width, 2 * ff), bf16),
            pltpu.VMEM((experts, ff, width), bf16),
            pltpu.VMEM((2, 2 * rows, width), bf16),
            pltpu.VMEM((blocks, rows, width), bf16),
            pltpu.VMEM((blocks, rows, width), bf16),
            pltpu.VMEM((blocks, rows, width), bf16),
            pltpu.VMEM((nz, 2, rows // 2, width), bf16),
            pltpu.VMEM((nz, rows, width), bf16),
            pltpu.VMEM((nz, rows, width), bf16),
            pltpu.VMEM((nz + 1, rows, width), bf16),
            dma((4,)), dma((2, 2)),
            dma((nz,)), dma((nz,)), dma((nz,)),
            dma((nz,)), dma((nz,)), dma((nz,)), dma((nz,)),
            dma((nz, 2)), dma((nz, 2)),
            dma((blocks,)), dma((blocks,)),
            dma((blocks,)), dma((blocks,)),
            dma((nz, 2)), dma((nz, 2)),
            dma((nz,)), dma((nz,)), dma((nz,)), dma((nz,)),
            dma((nz,)), dma((nz,)), dma((nz + 1,)),
        ],
        compiler_params=pltpu.CompilerParams(
            collective_id=0, has_side_effects=True, vmem_limit_bytes=60 * 2**20),
        cost_estimate=pl.CostEstimate(flops=12 * blocks * rows * width * ff,
                                      bytes_accessed=6 * experts * width * ff, transcendentals=0),
    )(tile_expert, slots, gate_weight, up_weight, down_weight)
    return (slot_weight[:, None] * summed).astype(bf16)


def fits(n, slots, gate_weight):
    rows, width = slots.shape
    experts, _, ff = gate_weight.shape
    blocks, nz = n // 2, n // 8
    held = experts * width * 3 * ff + (4 + 3 * blocks + 4 * nz + 3) * rows * width
    return (n % 8 == 0 and n >= 16 and 2 * rows == TILE and ff % 128 == 0 and width % 1024 == 0
            and 2 * held <= 57 * 2**20)


def solution(mesh):
    n = mesh.shape["loop"]
    in_specs = (
        P(("parts", "loop"), None),
        P("parts", None),
        P(("parts", "loop")),
        P(None, None, "loop"),
        P(None, None, "loop"),
        P(None, "loop", None),
    )
    out_specs = P(("parts", "loop"), None)

    def per_device(slots, tile_expert, slot_weight, gate_weight, up_weight, down_weight):
        args = (slots, tile_expert, slot_weight, gate_weight, up_weight, down_weight)
        if fits(n, slots, gate_weight):
            return kernel_form(n, *args)
        return collective_form(*args)

    return jax.shard_map(
        per_device, mesh=mesh, in_specs=in_specs, out_specs=out_specs, check_vma=False
    )
```

```python
import functools

import jax
import jax.numpy as jnp
from jax import lax
from jax.experimental import pallas as pl
from jax.experimental.pallas import tpu as pltpu
from jax.sharding import PartitionSpec as P

TILE = 128
MESH = pl.DeviceIdType.MESH
F32 = jnp.float32


def expert_part(row_block, chosen, gate_weight, up_weight, down_weight):
    gate_cols = lax.dynamic_index_in_dim(gate_weight, chosen, 0, keepdims=False)
    up_cols = lax.dynamic_index_in_dim(up_weight, chosen, 0, keepdims=False)
    down_rows = lax.dynamic_index_in_dim(down_weight, chosen, 0, keepdims=False)
    gate_value = jnp.dot(row_block, gate_cols, preferred_element_type=jnp.float32)
    up_value = jnp.dot(row_block, up_cols, preferred_element_type=jnp.float32)
    hidden = (jax.nn.silu(gate_value) * up_value).astype(jnp.bfloat16)
    return jnp.dot(hidden, down_rows, preferred_element_type=jnp.float32)


def collective_form(slots, tile_expert, slot_weight, gate_weight, up_weight, down_weight):
    chosen_ids = tile_expert[:, 0]
    width = slots.shape[1]
    gathered = lax.all_gather(slots, "loop", axis=0, tiled=True)
    tile_rows = gathered.reshape(-1, TILE, width)

    def expert_tile(operands):
        row_block, chosen = operands
        return expert_part(row_block, chosen, gate_weight, up_weight, down_weight)

    partial_value = lax.map(expert_tile, (tile_rows, chosen_ids)).reshape(-1, width)
    summed = lax.psum_scatter(partial_value, "loop", scatter_dimension=0, tiled=True)
    return (slot_weight[:, None] * summed).astype(jnp.bfloat16)


def kernel(nz, te, slots, gate, up, down, out, x, wgu, wd, xv, own, stage, sib, rd, rx, ry, rz,
           wsem, xsem, s_zu, s_zd, r_z, s_x, r_x, s_y, r_y, s_f, r_f, s_s, r_s,
           s_p, r_p, s_d, r_d, s_px, r_px, s_py, r_py, s_ru, s_rd, r_rz):
    rows, width = slots.shape
    half = rows // 2
    ff = gate.shape[2]
    me = lax.axis_index("loop")
    c = me % 2
    px = (me // 2) % 2
    py = (me // 4) % 2
    z = me // 8
    turn = 1 - 2 * ((2 * z) // nz)

    def chip(s, j):
        return (s * 2 + (py + j // 2) % 2) * 2 + (px + j % 2) % 2

    def device(s, j, core):
        return {"loop": chip(s, j) * 2 + core}

    xn, yn, sb = device(z, 1, c), device(z, 2, c), device(z, 0, 1 - c)

    def zdev(step):
        return {"loop": me + 8 * step}

    has_up, has_dn = z < nz - 1, z > 0

    def remote(src, dst, ssem, rsem, dev):
        return pltpu.make_async_remote_copy(src_ref=src, dst_ref=dst, send_sem=ssem, recv_sem=rsem,
                                            device_id=dev, device_id_type=MESH)

    def order(i):
        return (z + turn * i + nz) % nz

    def late(p):
        return (1 - p // 2) * (2 + p) + (p // 2) * (3 - p)

    def zu(q):
        b = x.at[chip(q, 0), c]
        return remote(b, b, s_zu.at[q], r_z.at[q], zdev(1))

    def zd(q):
        b = x.at[chip(q, 0), c]
        return remote(b, b, s_zd.at[q], r_z.at[q], zdev(-1))

    def gx(s):
        b = x.at[chip(s, 0), c]
        return remote(b, b, s_x.at[s], r_x.at[s], xn)

    def gy(s):
        b = x.at[chip(s, 0), c]
        return remote(b, b, s_y.at[s], r_y.at[s], yn)

    def fy(s):
        b = x.at[chip(s, 1), c, pl.ds(0, half)]
        return remote(b, b, s_f.at[s, 0], r_f.at[s, 0], yn)

    def fx(s):
        b = x.at[chip(s, 2), c, pl.ds(half, half)]
        return remote(b, b, s_f.at[s, 1], r_f.at[s, 1], xn)

    def gs(k):
        b = x.at[k, c]
        return remote(b, b, s_s.at[k], r_s.at[k], sb)

    def ps(k):
        return remote(stage.at[k], sib.at[k], s_p.at[k], r_p.at[k], sb)

    def dx(s):
        return remote(own.at[chip(s, 3), pl.ds(0, half)], rd.at[s, 0], s_d.at[s, 0], r_d.at[s, 0], xn)

    def dy(s):
        return remote(own.at[chip(s, 3), pl.ds(half, half)], rd.at[s, 1], s_d.at[s, 1], r_d.at[s, 1], yn)

    def sx(s):
        return remote(own.at[chip(s, 1)], rx.at[s], s_px.at[s], r_px.at[s], xn)

    def sy(s):
        return remote(own.at[chip(s, 2)], ry.at[s], s_py.at[s], r_py.at[s], yn)

    def ru(s):
        return remote(own.at[chip(s, 0)], rz.at[s], s_ru.at[s], r_rz.at[s], zdev(1))

    def rdn(s):
        slot = jnp.where(z - 1 == s, nz, s)
        return remote(own.at[chip(s, 0)], rz.at[slot], s_rd.at[s], r_rz.at[slot], zdev(-1))

    def rz_wait(slot):
        remote(rz.at[slot], rz.at[slot], s_ru.at[0], r_rz.at[slot], zdev(0)).wait_recv()

    mine = chip(z, 0)
    first = pltpu.make_async_copy(slots, x.at[mine, c], wsem.at[0])
    first.start()
    loads = [
        pltpu.make_async_copy(gate, wgu.at[:, :, pl.ds(0, ff)], wsem.at[1]),
        pltpu.make_async_copy(up, wgu.at[:, :, pl.ds(ff, ff)], wsem.at[2]),
        pltpu.make_async_copy(down, wd, wsem.at[3]),
    ]

    barrier = pltpu.get_barrier_semaphore()
    for dev in (sb, xn, yn):
        pl.semaphore_signal(barrier, inc=1, device_id=dev, device_id_type=MESH)

    @pl.when(has_up)
    def _():
        pl.semaphore_signal(barrier, inc=1, device_id=zdev(1), device_id_type=MESH)

    @pl.when(has_dn)
    def _():
        pl.semaphore_signal(barrier, inc=1, device_id=zdev(-1), device_id_type=MESH)

    pl.semaphore_wait(barrier, 3 + has_up.astype(jnp.int32) + has_dn.astype(jnp.int32))
    first.wait()

    def z_send(q, going_up):
        @pl.when(has_up if going_up else has_dn)
        def _():
            (zu if going_up else zd)(q).start()

    def stage_z(t):
        low, high = z - t, z + t

        @pl.when(low >= 0)
        def _():
            zu(low).wait_recv()
            z_send(low, True)

        @pl.when(high < nz)
        def _():
            zd(high).wait_recv()
            z_send(high, False)

    def stage_a(i):
        s = order(i)
        gx(s).start()
        gy(s).start()
        gs(chip(s, 0)).start()

    def stage_b(i):
        s = order(i)
        remote(x.at[chip(s, 1), c], x.at[chip(s, 1), c], s_x.at[s], r_x.at[s], xn).wait_recv()
        fy(s).start()
        gs(chip(s, 1)).start()
        remote(x.at[chip(s, 2), c], x.at[chip(s, 2), c], s_y.at[s], r_y.at[s], yn).wait_recv()
        fx(s).start()
        gs(chip(s, 2)).start()

    def stage_c(i):
        s = order(i)
        k = chip(s, 3)
        for h in range(2):
            b = x.at[k, c, pl.ds(h * half, half)]
            remote(b, b, s_f.at[s, h], r_f.at[s, h], xn).wait_recv()
        gs(k).start()

    def load(s, j):
        k, slot = chip(s, j), j % 2
        return [pltpu.make_async_copy(x.at[k, c], xv.at[slot, pl.ds(0, rows)], xsem.at[slot, 0]),
                pltpu.make_async_copy(x.at[k, 1 - c], xv.at[slot, pl.ds(rows, rows)], xsem.at[slot, 1])]

    def fetch(s, j):
        b = x.at[chip(s, j), 1 - c]
        remote(b, b, s_s.at[0], r_s.at[chip(s, j)], sb).wait_recv()
        for cp in load(s, j):
            cp.start()

    def stage_d(i):
        s = order(i)
        fetch(s, 0)

        def block(j, carry):
            @pl.when(j < 3)
            def _():
                fetch(s, j + 1)

            for cp in load(s, j):
                cp.wait()
            k, slot = chip(s, j), j % 2
            e = te[k, 0]
            step = min(width, 1024)
            acc = jnp.zeros((2 * rows, 2 * ff), F32)
            for k0 in range(0, width, step):
                acc += jnp.dot(xv[slot, :, k0:k0 + step], wgu[e, k0:k0 + step, :],
                               preferred_element_type=F32)
            hidden = (jax.nn.silu(acc[:, :ff]) * acc[:, ff:]).astype(jnp.bfloat16)
            for n0 in range(0, width, step):
                part = jnp.dot(hidden, wd[e, :, n0:n0 + step], preferred_element_type=F32)
                part = part.astype(jnp.bfloat16)
                own[k, :, n0:n0 + step] = part[:rows]
                stage[k, :, n0:n0 + step] = part[rows:]
            ps(k).start()
            return carry

        lax.fori_loop(0, 4, block, 0)

    def add_rows(start, count, dst, *terms):
        step = min(width, 1024)

        def rows16(t, carry):
            r = pl.ds(start + t * 16, 16)
            for n0 in range(0, width, step):
                n = slice(n0, n0 + step)
                total = dst[r, n].astype(F32)
                for ref, shift in terms:
                    total += ref[pl.ds(start - shift + t * 16, 16), n].astype(F32)
                dst[r, n] = total.astype(dst.dtype)
            return carry

        lax.fori_loop(0, count // 16, rows16, 0)

    def stage_r1(i):
        s = order(i)
        for j in (3, 2, 1, 0):
            ps(chip(s, j)).wait_recv()
        k = chip(s, 3)
        add_rows(0, rows, own.at[k], (sib.at[k], 0))
        dx(s).start()
        dy(s).start()

    def stage_r2(i):
        s = order(i)
        kx, ky = chip(s, 1), chip(s, 2)
        dx(s).wait_recv()
        add_rows(0, half, own.at[ky], (sib.at[ky], 0), (rd.at[s, 0], 0))
        add_rows(half, half, own.at[ky], (sib.at[ky], 0))
        sy(s).start()
        dy(s).wait_recv()
        add_rows(0, half, own.at[kx], (sib.at[kx], 0))
        add_rows(half, half, own.at[kx], (sib.at[kx], 0), (rd.at[s, 1], half))
        sx(s).start()

    def stage_r3(i):
        s = order(i)
        k = chip(s, 0)
        sx(s).wait_recv()
        sy(s).wait_recv()
        add_rows(0, rows, own.at[k], (sib.at[k], 0), (rx.at[s], 0), (ry.at[s], 0))

        @pl.when(jnp.logical_and(s > z, jnp.logical_not(has_dn)))
        def _():
            ru(s).start()

        @pl.when(jnp.logical_and(s < z, jnp.logical_not(has_up)))
        def _():
            rdn(s).start()

    def stage_r4(i):
        s = order(i)
        k = chip(s, 0)

        @pl.when(jnp.logical_and(s > z, has_dn))
        def _():
            rz_wait(s)
            add_rows(0, rows, own.at[k], (rz.at[s], 0))
            ru(s).start()

        @pl.when(jnp.logical_and(s < z, has_up))
        def _():
            rz_wait(s)
            add_rows(0, rows, own.at[k], (rz.at[s], 0))
            rdn(s).start()

        @pl.when(s == z)
        def _():
            @pl.when(has_dn)
            def _():
                rz_wait(s)

            @pl.when(has_up)
            def _():
                rz_wait(nz)

            out[...] = jnp.zeros((rows, width), F32)
            add_rows(0, rows, out, (own.at[k], 0), (rz.at[s], 0), (rz.at[nz], 0))

    z_send(z, True)
    z_send(z, False)
    stage_a(0)
    for cp in loads:
        cp.start()

    @pl.when(jnp.logical_not(has_dn))
    def _():
        rz[0] = jnp.zeros((rows, width), jnp.bfloat16)

    @pl.when(jnp.logical_not(has_up))
    def _():
        rz[nz] = jnp.zeros((rows, width), jnp.bfloat16)

    stage_z(1)
    stage_a(1)
    stage_b(0)

    def body(n, carry):
        @pl.when(n + 2 < nz)
        def _():
            stage_z(n + 2)
            stage_a(n + 2)

        @pl.when(n < nz)
        def _():
            stage_c(n)

        @pl.when(n + 1 < nz)
        def _():
            stage_b(n + 1)

        @pl.when(n == 0)
        def _():
            for cp in loads:
                cp.wait()

        @pl.when(n == 3)
        def _():
            stage_r2(late(0))

        @pl.when(n < nz)
        def _():
            stage_d(n)

        @pl.when(n < nz)
        def _():
            stage_r1(n)

        @pl.when(jnp.logical_and(n >= 3, n <= 5))
        def _():
            stage_r2(late(n - 2))

        @pl.when(jnp.logical_and(n >= 4, n <= 7))
        def _():
            stage_r3(late(n - 4))

        @pl.when(n >= 6)
        def _():
            stage_r4(late(n - 6))

        return carry

    lax.fori_loop(0, 10, body, 0)

    def finish(q, carry):
        for cp in (gx(q), gy(q), fx(q), fy(q), dx(q), dy(q), sx(q), sy(q)):
            cp.wait_send()

        @pl.when(jnp.logical_and(has_up, q <= z))
        def _():
            zu(q).wait_send()

        @pl.when(jnp.logical_and(has_dn, q >= z))
        def _():
            zd(q).wait_send()

        @pl.when(q > z)
        def _():
            ru(q).wait_send()

        @pl.when(q < z)
        def _():
            rdn(q).wait_send()

        return carry

    lax.fori_loop(0, nz, finish, 0)

    def finish_pair(k, carry):
        gs(k).wait_send()
        ps(k).wait_send()
        return carry

    lax.fori_loop(0, 4 * nz, finish_pair, 0)


def kernel_form(n, slots, tile_expert, slot_weight, gate_weight, up_weight, down_weight):
    nz, blocks = n // 8, n // 2
    rows, width = slots.shape
    experts, _, ff = gate_weight.shape
    bf16 = jnp.bfloat16
    dma = pltpu.SemaphoreType.DMA
    anywhere = pl.BlockSpec(memory_space=pl.ANY)
    summed, _ = pl.pallas_call(
        functools.partial(kernel, nz),
        out_shape=(jax.ShapeDtypeStruct((rows, width), F32),
                   jax.ShapeDtypeStruct((blocks, 2, rows, width), bf16)),
        in_specs=[pl.BlockSpec(memory_space=pltpu.SMEM), pl.BlockSpec(memory_space=pltpu.VMEM)]
        + [anywhere] * 3,
        out_specs=(pl.BlockSpec(memory_space=pltpu.VMEM), anywhere),
        scratch_shapes=[
            pltpu.VMEM((experts, width, 2 * ff), bf16),
            pltpu.VMEM((experts, ff, width), bf16),
            pltpu.VMEM((2, 2 * rows, width), bf16),
            pltpu.VMEM((blocks, rows, width), bf16),
            pltpu.VMEM((blocks, rows, width), bf16),
            pltpu.VMEM((blocks, rows, width), bf16),
            pltpu.VMEM((nz, 2, rows // 2, width), bf16),
            pltpu.VMEM((nz, rows, width), bf16),
            pltpu.VMEM((nz, rows, width), bf16),
            pltpu.VMEM((nz + 1, rows, width), bf16),
            dma((4,)), dma((2, 2)),
            dma((nz,)), dma((nz,)), dma((nz,)),
            dma((nz,)), dma((nz,)), dma((nz,)), dma((nz,)),
            dma((nz, 2)), dma((nz, 2)),
            dma((blocks,)), dma((blocks,)),
            dma((blocks,)), dma((blocks,)),
            dma((nz, 2)), dma((nz, 2)),
            dma((nz,)), dma((nz,)), dma((nz,)), dma((nz,)),
            dma((nz,)), dma((nz,)), dma((nz + 1,)),
        ],
        compiler_params=pltpu.CompilerParams(
            collective_id=0, has_side_effects=True, vmem_limit_bytes=60 * 2**20),
        cost_estimate=pl.CostEstimate(flops=12 * blocks * rows * width * ff,
                                      bytes_accessed=6 * experts * width * ff, transcendentals=0),
    )(tile_expert, slots, gate_weight, up_weight, down_weight)
    return (slot_weight[:, None] * summed).astype(bf16)


def fits(n, slots, gate_weight):
    rows, width = slots.shape
    experts, _, ff = gate_weight.shape
    blocks, nz = n // 2, n // 8
    held = experts * width * 3 * ff + (4 + 3 * blocks + 4 * nz + 3) * rows * width
    return (n == 32 and 2 * rows == TILE and ff % 128 == 0 and width % 1024 == 0
            and 2 * held <= 57 * 2**20)


def solution(mesh):
    n = mesh.shape["loop"]
    in_specs = (
        P(("parts", "loop"), None),
        P("parts", None),
        P(("parts", "loop")),
        P(None, None, "loop"),
        P(None, None, "loop"),
        P(None, "loop", None),
    )
    out_specs = P(("parts", "loop"), None)

    def per_device(slots, tile_expert, slot_weight, gate_weight, up_weight, down_weight):
        args = (slots, tile_expert, slot_weight, gate_weight, up_weight, down_weight)
        if fits(n, slots, gate_weight):
            return kernel_form(n, *args)
        return collective_form(*args)

    return jax.shard_map(
        per_device, mesh=mesh, in_specs=in_specs, out_specs=out_specs, check_vma=False
    )
```

```python
import functools

import jax
import jax.numpy as jnp
from jax import lax
from jax.experimental import pallas as pl
from jax.experimental.pallas import tpu as pltpu
from jax.sharding import PartitionSpec as P

TILE = 128
MESH = pl.DeviceIdType.MESH
F32 = jnp.float32


def expert_part(row_block, chosen, gate_weight, up_weight, down_weight):
    gate_cols = lax.dynamic_index_in_dim(gate_weight, chosen, 0, keepdims=False)
    up_cols = lax.dynamic_index_in_dim(up_weight, chosen, 0, keepdims=False)
    down_rows = lax.dynamic_index_in_dim(down_weight, chosen, 0, keepdims=False)
    gate_value = jnp.dot(row_block, gate_cols, preferred_element_type=jnp.float32)
    up_value = jnp.dot(row_block, up_cols, preferred_element_type=jnp.float32)
    hidden = (jax.nn.silu(gate_value) * up_value).astype(jnp.bfloat16)
    return jnp.dot(hidden, down_rows, preferred_element_type=jnp.float32)


def collective_form(slots, tile_expert, slot_weight, gate_weight, up_weight, down_weight):
    chosen_ids = tile_expert[:, 0]
    width = slots.shape[1]
    gathered = lax.all_gather(slots, "loop", axis=0, tiled=True)
    tile_rows = gathered.reshape(-1, TILE, width)

    def expert_tile(operands):
        row_block, chosen = operands
        return expert_part(row_block, chosen, gate_weight, up_weight, down_weight)

    partial_value = lax.map(expert_tile, (tile_rows, chosen_ids)).reshape(-1, width)
    summed = lax.psum_scatter(partial_value, "loop", scatter_dimension=0, tiled=True)
    return (slot_weight[:, None] * summed).astype(jnp.bfloat16)


def kernel(nz, te, slots, gate, up, down, out, x, wgu, wd, xv, own, stage, sib, rd, rx, ry, rz,
           wsem, xsem, s_zu, s_zd, r_z, s_x, r_x, s_y, r_y, s_f, r_f, s_s, r_s,
           s_p, r_p, s_d, r_d, s_px, r_px, s_py, r_py, s_ru, s_rd, r_rz):
    rows, width = slots.shape
    half = rows // 2
    ff = gate.shape[2]
    me = lax.axis_index("loop")
    c = me % 2
    px = (me // 2) % 2
    py = (me // 4) % 2
    z = me // 8
    turn = 1 - 2 * ((2 * z) // nz)

    def chip(s, j):
        return (s * 2 + (py + j // 2) % 2) * 2 + (px + j % 2) % 2

    def device(s, j, core):
        return {"loop": chip(s, j) * 2 + core}

    xn, yn, sb = device(z, 1, c), device(z, 2, c), device(z, 0, 1 - c)

    def zdev(step):
        return {"loop": me + 8 * step}

    has_up, has_dn = z < nz - 1, z > 0

    def remote(src, dst, ssem, rsem, dev):
        return pltpu.make_async_remote_copy(src_ref=src, dst_ref=dst, send_sem=ssem, recv_sem=rsem,
                                            device_id=dev, device_id_type=MESH)

    def order(i):
        return (z + turn * i + nz) % nz

    def late(p):
        return (1 - p // 2) * (2 + p) + (p // 2) * (3 - p)

    def zu(q):
        b = x.at[chip(q, 0), c]
        return remote(b, b, s_zu.at[q], r_z.at[q], zdev(1))

    def zd(q):
        b = x.at[chip(q, 0), c]
        return remote(b, b, s_zd.at[q], r_z.at[q], zdev(-1))

    def gx(s):
        b = x.at[chip(s, 0), c]
        return remote(b, b, s_x.at[s], r_x.at[s], xn)

    def gy(s):
        b = x.at[chip(s, 0), c]
        return remote(b, b, s_y.at[s], r_y.at[s], yn)

    def fy(s):
        b = x.at[chip(s, 1), c, pl.ds(0, half)]
        return remote(b, b, s_f.at[s, 0], r_f.at[s, 0], yn)

    def fx(s):
        b = x.at[chip(s, 2), c, pl.ds(half, half)]
        return remote(b, b, s_f.at[s, 1], r_f.at[s, 1], xn)

    def gs(k):
        b = x.at[k, c]
        return remote(b, b, s_s.at[k], r_s.at[k], sb)

    def ps(k):
        return remote(stage.at[k], sib.at[k], s_p.at[k], r_p.at[k], sb)

    def dx(s):
        return remote(own.at[chip(s, 3), pl.ds(0, half)], rd.at[s, 0], s_d.at[s, 0], r_d.at[s, 0], xn)

    def dy(s):
        return remote(own.at[chip(s, 3), pl.ds(half, half)], rd.at[s, 1], s_d.at[s, 1], r_d.at[s, 1], yn)

    def sx(s):
        return remote(own.at[chip(s, 1)], rx.at[s], s_px.at[s], r_px.at[s], xn)

    def sy(s):
        return remote(own.at[chip(s, 2)], ry.at[s], s_py.at[s], r_py.at[s], yn)

    def ru(s):
        return remote(own.at[chip(s, 0)], rz.at[s], s_ru.at[s], r_rz.at[s], zdev(1))

    def rdn(s):
        slot = jnp.where(z - 1 == s, nz, s)
        return remote(own.at[chip(s, 0)], rz.at[slot], s_rd.at[s], r_rz.at[slot], zdev(-1))

    def rz_wait(slot):
        remote(rz.at[slot], rz.at[slot], s_ru.at[0], r_rz.at[slot], zdev(0)).wait_recv()

    mine = chip(z, 0)
    first = pltpu.make_async_copy(slots, x.at[mine, c], wsem.at[0])
    first.start()
    loads = [
        pltpu.make_async_copy(gate, wgu.at[:, :, pl.ds(0, ff)], wsem.at[1]),
        pltpu.make_async_copy(up, wgu.at[:, :, pl.ds(ff, ff)], wsem.at[2]),
        pltpu.make_async_copy(down, wd, wsem.at[3]),
    ]

    barrier = pltpu.get_barrier_semaphore()
    for dev in (sb, xn, yn):
        pl.semaphore_signal(barrier, inc=1, device_id=dev, device_id_type=MESH)

    @pl.when(has_up)
    def _():
        pl.semaphore_signal(barrier, inc=1, device_id=zdev(1), device_id_type=MESH)

    @pl.when(has_dn)
    def _():
        pl.semaphore_signal(barrier, inc=1, device_id=zdev(-1), device_id_type=MESH)

    pl.semaphore_wait(barrier, 3 + has_up.astype(jnp.int32) + has_dn.astype(jnp.int32))
    first.wait()

    def z_send(q, going_up):
        @pl.when(has_up if going_up else has_dn)
        def _():
            (zu if going_up else zd)(q).start()

    def stage_z(t):
        low, high = z - t, z + t

        @pl.when(low >= 0)
        def _():
            zu(low).wait_recv()
            z_send(low, True)

        @pl.when(high < nz)
        def _():
            zd(high).wait_recv()
            z_send(high, False)

    def stage_a(i):
        s = order(i)
        gx(s).start()
        gy(s).start()
        gs(chip(s, 0)).start()

    def stage_b(i):
        s = order(i)
        remote(x.at[chip(s, 1), c], x.at[chip(s, 1), c], s_x.at[s], r_x.at[s], xn).wait_recv()
        fy(s).start()
        gs(chip(s, 1)).start()
        remote(x.at[chip(s, 2), c], x.at[chip(s, 2), c], s_y.at[s], r_y.at[s], yn).wait_recv()
        fx(s).start()
        gs(chip(s, 2)).start()

    def stage_c(i):
        s = order(i)
        k = chip(s, 3)
        for h in range(2):
            b = x.at[k, c, pl.ds(h * half, half)]
            remote(b, b, s_f.at[s, h], r_f.at[s, h], xn).wait_recv()
        gs(k).start()

    def load(s, j):
        k, slot = chip(s, j), j % 2
        return [pltpu.make_async_copy(x.at[k, c], xv.at[slot, pl.ds(0, rows)], xsem.at[slot, 0]),
                pltpu.make_async_copy(x.at[k, 1 - c], xv.at[slot, pl.ds(rows, rows)], xsem.at[slot, 1])]

    def fetch(s, j):
        b = x.at[chip(s, j), 1 - c]
        remote(b, b, s_s.at[0], r_s.at[chip(s, j)], sb).wait_recv()
        for cp in load(s, j):
            cp.start()

    def stage_d(i):
        s = order(i)
        fetch(s, 0)

        def block(j, carry):
            @pl.when(j < 3)
            def _():
                fetch(s, j + 1)

            for cp in load(s, j):
                cp.wait()
            k, slot = chip(s, j), j % 2
            e = te[k, 0]
            step = min(width, 1024)
            acc = jnp.zeros((2 * rows, 2 * ff), F32)
            for k0 in range(0, width, step):
                acc += jnp.dot(xv[slot, :, k0:k0 + step], wgu[e, k0:k0 + step, :],
                               preferred_element_type=F32)
            hidden = (jax.nn.silu(acc[:, :ff]) * acc[:, ff:]).astype(jnp.bfloat16)
            for n0 in range(0, width, step):
                part = jnp.dot(hidden, wd[e, :, n0:n0 + step], preferred_element_type=F32)
                part = part.astype(jnp.bfloat16)
                own[k, :, n0:n0 + step] = part[:rows]
                stage[k, :, n0:n0 + step] = part[rows:]
            ps(k).start()
            return carry

        lax.fori_loop(0, 4, block, 0)

    def add_rows(start, count, dst, *terms):
        step = min(width, 1024)

        def rows16(t, carry):
            r = pl.ds(start + t * 16, 16)
            for n0 in range(0, width, step):
                n = slice(n0, n0 + step)
                total = dst[r, n].astype(F32)
                for ref, shift in terms:
                    total += ref[pl.ds(start - shift + t * 16, 16), n].astype(F32)
                dst[r, n] = total.astype(dst.dtype)
            return carry

        lax.fori_loop(0, count // 16, rows16, 0)

    def stage_r1(i):
        s = order(i)
        for j in (3, 2, 1, 0):
            ps(chip(s, j)).wait_recv()
        k = chip(s, 3)
        add_rows(0, rows, own.at[k], (sib.at[k], 0))
        dx(s).start()
        dy(s).start()

    def stage_r2(i):
        s = order(i)
        kx, ky = chip(s, 1), chip(s, 2)
        dx(s).wait_recv()
        add_rows(0, half, own.at[ky], (sib.at[ky], 0), (rd.at[s, 0], 0))
        add_rows(half, half, own.at[ky], (sib.at[ky], 0))
        sy(s).start()
        dy(s).wait_recv()
        add_rows(0, half, own.at[kx], (sib.at[kx], 0))
        add_rows(half, half, own.at[kx], (sib.at[kx], 0), (rd.at[s, 1], half))
        sx(s).start()

    def stage_r3(i):
        s = order(i)
        k = chip(s, 0)
        sx(s).wait_recv()
        sy(s).wait_recv()
        add_rows(0, rows, own.at[k], (sib.at[k], 0), (rx.at[s], 0), (ry.at[s], 0))

        @pl.when(jnp.logical_and(s > z, jnp.logical_not(has_dn)))
        def _():
            ru(s).start()

        @pl.when(jnp.logical_and(s < z, jnp.logical_not(has_up)))
        def _():
            rdn(s).start()

    def stage_r4(i):
        s = order(i)
        k = chip(s, 0)

        @pl.when(jnp.logical_and(s > z, has_dn))
        def _():
            rz_wait(s)
            add_rows(0, rows, own.at[k], (rz.at[s], 0))
            ru(s).start()

        @pl.when(jnp.logical_and(s < z, has_up))
        def _():
            rz_wait(s)
            add_rows(0, rows, own.at[k], (rz.at[s], 0))
            rdn(s).start()

        @pl.when(s == z)
        def _():
            @pl.when(has_dn)
            def _():
                rz_wait(s)

            @pl.when(has_up)
            def _():
                rz_wait(nz)

            out[...] = jnp.zeros((rows, width), F32)
            add_rows(0, rows, out, (own.at[k], 0), (rz.at[s], 0), (rz.at[nz], 0))

    z_send(z, True)
    z_send(z, False)
    stage_a(0)
    for cp in loads:
        cp.start()

    @pl.when(jnp.logical_not(has_dn))
    def _():
        rz[0] = jnp.zeros((rows, width), jnp.bfloat16)

    @pl.when(jnp.logical_not(has_up))
    def _():
        rz[nz] = jnp.zeros((rows, width), jnp.bfloat16)

    stage_z(1)
    stage_a(1)
    stage_b(0)

    def body(n, carry):
        @pl.when(n + 2 < nz)
        def _():
            stage_z(n + 2)
            stage_a(n + 2)

        @pl.when(n < nz)
        def _():
            stage_c(n)

        @pl.when(n + 1 < nz)
        def _():
            stage_b(n + 1)

        @pl.when(n == 0)
        def _():
            for cp in loads:
                cp.wait()

        @pl.when(n == 3)
        def _():
            stage_r2(late(0))

        @pl.when(n < nz)
        def _():
            stage_d(n)

        @pl.when(n < nz)
        def _():
            stage_r1(n)

        @pl.when(jnp.logical_and(n >= 3, n <= 5))
        def _():
            stage_r2(late(n - 2))

        @pl.when(jnp.logical_and(n >= 4, n <= 7))
        def _():
            stage_r3(late(n - 4))

        @pl.when(n >= 5)
        def _():
            stage_r4(late(n - 5))

        return carry

    lax.fori_loop(0, 9, body, 0)

    def finish(q, carry):
        for cp in (gx(q), gy(q), fx(q), fy(q), dx(q), dy(q), sx(q), sy(q)):
            cp.wait_send()

        @pl.when(jnp.logical_and(has_up, q <= z))
        def _():
            zu(q).wait_send()

        @pl.when(jnp.logical_and(has_dn, q >= z))
        def _():
            zd(q).wait_send()

        @pl.when(q > z)
        def _():
            ru(q).wait_send()

        @pl.when(q < z)
        def _():
            rdn(q).wait_send()

        return carry

    lax.fori_loop(0, nz, finish, 0)

    def finish_pair(k, carry):
        gs(k).wait_send()
        ps(k).wait_send()
        return carry

    lax.fori_loop(0, 4 * nz, finish_pair, 0)


def kernel_form(n, slots, tile_expert, slot_weight, gate_weight, up_weight, down_weight):
    nz, blocks = n // 8, n // 2
    rows, width = slots.shape
    experts, _, ff = gate_weight.shape
    bf16 = jnp.bfloat16
    dma = pltpu.SemaphoreType.DMA
    anywhere = pl.BlockSpec(memory_space=pl.ANY)
    summed, _ = pl.pallas_call(
        functools.partial(kernel, nz),
        out_shape=(jax.ShapeDtypeStruct((rows, width), F32),
                   jax.ShapeDtypeStruct((blocks, 2, rows, width), bf16)),
        in_specs=[pl.BlockSpec(memory_space=pltpu.SMEM), pl.BlockSpec(memory_space=pltpu.VMEM)]
        + [anywhere] * 3,
        out_specs=(pl.BlockSpec(memory_space=pltpu.VMEM), anywhere),
        scratch_shapes=[
            pltpu.VMEM((experts, width, 2 * ff), bf16),
            pltpu.VMEM((experts, ff, width), bf16),
            pltpu.VMEM((2, 2 * rows, width), bf16),
            pltpu.VMEM((blocks, rows, width), bf16),
            pltpu.VMEM((blocks, rows, width), bf16),
            pltpu.VMEM((blocks, rows, width), bf16),
            pltpu.VMEM((nz, 2, rows // 2, width), bf16),
            pltpu.VMEM((nz, rows, width), bf16),
            pltpu.VMEM((nz, rows, width), bf16),
            pltpu.VMEM((nz + 1, rows, width), bf16),
            dma((4,)), dma((2, 2)),
            dma((nz,)), dma((nz,)), dma((nz,)),
            dma((nz,)), dma((nz,)), dma((nz,)), dma((nz,)),
            dma((nz, 2)), dma((nz, 2)),
            dma((blocks,)), dma((blocks,)),
            dma((blocks,)), dma((blocks,)),
            dma((nz, 2)), dma((nz, 2)),
            dma((nz,)), dma((nz,)), dma((nz,)), dma((nz,)),
            dma((nz,)), dma((nz,)), dma((nz + 1,)),
        ],
        compiler_params=pltpu.CompilerParams(
            collective_id=0, has_side_effects=True, vmem_limit_bytes=60 * 2**20),
        cost_estimate=pl.CostEstimate(flops=12 * blocks * rows * width * ff,
                                      bytes_accessed=6 * experts * width * ff, transcendentals=0),
    )(tile_expert, slots, gate_weight, up_weight, down_weight)
    return (slot_weight[:, None] * summed).astype(bf16)


def fits(n, slots, gate_weight):
    rows, width = slots.shape
    experts, _, ff = gate_weight.shape
    blocks, nz = n // 2, n // 8
    held = experts * width * 3 * ff + (4 + 3 * blocks + 4 * nz + 3) * rows * width
    return (n == 32 and 2 * rows == TILE and ff % 128 == 0 and width % 1024 == 0
            and 2 * held <= 57 * 2**20)


def solution(mesh):
    n = mesh.shape["loop"]
    in_specs = (
        P(("parts", "loop"), None),
        P("parts", None),
        P(("parts", "loop")),
        P(None, None, "loop"),
        P(None, None, "loop"),
        P(None, "loop", None),
    )
    out_specs = P(("parts", "loop"), None)

    def per_device(slots, tile_expert, slot_weight, gate_weight, up_weight, down_weight):
        args = (slots, tile_expert, slot_weight, gate_weight, up_weight, down_weight)
        if fits(n, slots, gate_weight):
            return kernel_form(n, *args)
        return collective_form(*args)

    return jax.shard_map(
        per_device, mesh=mesh, in_specs=in_specs, out_specs=out_specs, check_vma=False
    )
```
